32 devices in a mesh: groups: 2 (over y), tensor: 4 (over z), dp: 2 (over x), section: 2 (over core).
Axes of the slice: x: 2, y: 2, z: 4, core: 2. Of those that a mesh axis runs over, the one named last changes fastest.
Arguments:
- queries: bfloat16 [8, 256, 16384], P('groups', 'tensor', ('dp', 'section')), parts along dimension 0, may hold values from -128 to 128
- cache: bfloat16 [4, 8, 256, 256, 128], P('groups', ('dp', 'section'), 'tensor'), parts along dimension 0, may hold values from -6 to 6
- fresh_kv: bfloat16 [8, 2, 8, 256, 128], P('groups', None, ('dp', 'section'), 'tensor'), parts along dimension 0, may hold values from -6 to 6
- lengths: int32 [512], P(('groups', 'tensor')), parts along dimension 0, may hold values from 1 to 256, as said below
- w_out: bfloat16 [16384, 16384], P(('dp', 'section'), 'tensor'), may hold values from -0.375 to 0.375
- residual: bfloat16 [8, 256, 16384], P('groups', ('dp', 'section'), 'tensor'), parts along dimension 0, may hold values from -4 to 4
- layers: bfloat16 [4, 4, 256, 16384], P('groups', None, ('dp', 'section'), 'tensor'), parts along dimension 0, may hold values from -6 to 6
- accepted: int32 [8, 256], P('groups', 'dp'), parts along dimension 0, may hold values from 0 to 1, as said below
- down_map: bfloat16 [3, 16384, 256], P(None, ('tensor', 'section')), may hold values from -0.02734375 to 0.02734375
- up_map: bfloat16 [256, 16384], P(None, ('tensor', 'section')), may hold values from -0.0234375 to 0.0234375
Outputs:
- top_hidden: bfloat16 [8, 256, 16384], P('groups', ('dp', 'section'), 'tensor'), parts along dimension 0
- grad_down: bfloat16 [6, 16384, 256], P('groups', ('tensor', 'section')), parts along dimension 0
- grad_up: bfloat16 [512, 16384], P('groups', ('tensor', 'section')), parts along dimension 0
The draws below stay inside these ranges and needn't reach their ends.
There are 2 independent parts, one for each index of `groups`. The reference program is written for one: setup_inputs(seed, part) draws one part's arguments, and reference() takes and returns one part's arrays. A program takes and returns all parts, laid end to end along the dimension named above; an argument that names none is the same for every part. Nothing has to cross between parts.
Inputs may be any that keep to these rules, and one draw needn't show every extreme that they name: `accepted`: in each decode step every aligned block of the step's rows that one dp and section index holds in the tables' layout of residual accepts 1 to 24 rows, and some block of each step accepts exactly 24. `lengths`: some row's cache is full.
All inputs are finite; a program needn't handle non-finite values.
Results may differ from the reference program's by a relative error of at most 0.012.
Values may be sent and summed in bfloat16 or wider, within the bound.
A program may use at most 256 MiB of HBM per device.

```python
import math
import jax
import jax.numpy as jnp
from jax import lax

D = 16384
HEADS = 128
HEAD_DIM = 128
KV_HEADS = 8
ROWS = 256
CACHE = 256
STEPS = 4
MOST = 24
RANK = 256
N_DP = 2
N_SECTION = 2


def cache_base(key):
    base = jax.random.normal(key, (2, KV_HEADS, ROWS, CACHE, HEAD_DIM), jnp.float32)
    return jnp.clip(base, -6.0, 6.0)


def draw_cache(key, part):
    base = cache_base(key)
    return base.astype(jnp.bfloat16)


def draw_queries(key, part):
    key = jax.random.fold_in(key, 5)
    query_rows = jax.random.normal(key, (STEPS, ROWS, HEADS, HEAD_DIM), jnp.float32)
    query_rows = jnp.clip(query_rows, -6.0, 6.0)
    return query_rows.reshape(STEPS, ROWS, HEADS * HEAD_DIM).astype(jnp.bfloat16)


def draw_lengths(key, part):
    key = jax.random.fold_in(key, 7)
    spans = jax.random.randint(key, (ROWS,), 1, CACHE + 1)
    spot = jax.random.randint(jax.random.fold_in(key, 1), (), 0, ROWS)
    return jnp.where(jnp.arange(ROWS) == spot, CACHE, spans).astype(jnp.int32)


def draw_accepted(key, part):
    key = jax.random.fold_in(key, 9)
    blocks = N_DP * N_SECTION
    width = ROWS // blocks
    counts = jax.random.randint(jax.random.fold_in(key, 1), (STEPS, blocks), 1, MOST + 1)
    forced = jax.random.randint(jax.random.fold_in(key, 2), (STEPS,), 0, blocks)
    counts = jnp.where(jnp.arange(blocks)[None, :] == forced[:, None], MOST, counts)
    keys = jax.random.split(jax.random.fold_in(key, 3), STEPS * blocks)
    ranks = jax.vmap(lambda single: jax.random.permutation(single, width))(keys)
    ranks = ranks.reshape(STEPS, blocks, width)
    chosen = (ranks < counts[..., None]).astype(jnp.int32)
    return chosen.reshape(STEPS, ROWS)


def block_levels(key, dims, shards, low, top_value):
    def one(dim, parts):
        draws = jax.random.uniform(jax.random.fold_in(jax.random.fold_in(key, 6), dim), (parts,), jnp.float32, low / len(shards), top_value / len(shards))
        return jnp.repeat(jnp.exp(draws), dims[dim] // parts).reshape((-1,) + (1,) * (len(dims) - dim - 1))

    factor_of = one(*shards[0])
    for cut in shards[1:]:
        factor_of = factor_of * one(*cut)
    return factor_of


def gaussian(stream_key, shape, spread, limit, pieces=(), kind=jnp.bfloat16):
    result = jax.random.normal(stream_key, shape, jnp.float32) * spread
    if len(pieces) > 0:
        result = block_levels(stream_key, shape, pieces, -0.22, 0.18) * result
    return jnp.clip(result, min=-limit, max=limit).astype(kind)


def setup_inputs(seed: int = 0, part: int = 0) -> dict:
    streams_of = jax.random.split(jax.random.key(seed), 11)
    part_splits = jax.random.split(jax.random.fold_in(streams_of[10], part), 11)
    return {
        "queries": draw_queries(jax.random.fold_in(jax.random.fold_in(streams_of[10], part), 71), part),
        "cache": draw_cache(jax.random.fold_in(jax.random.fold_in(streams_of[10], part), 71), part),
        "fresh_kv": gaussian(part_splits[2], (STEPS, 2, KV_HEADS, ROWS, HEAD_DIM), 1.0, 6.0, ((2, 4), (3, 4))),
        "lengths": draw_lengths(jax.random.fold_in(jax.random.fold_in(streams_of[10], part), 71), part),
        "w_out": gaussian(streams_of[4], (HEADS * HEAD_DIM, D), (HEADS * HEAD_DIM // 64) ** -0.5, 0.375, ((0, 4), (1, 4))),
        "residual": gaussian(part_splits[5], (STEPS, ROWS, D), 0.5, 4.0, ((1, 4), (2, 4))),
        "layers": gaussian(part_splits[6], (2, STEPS, ROWS, D), 1.0, 6.0, ((2, 4), (3, 4))),
        "accepted": draw_accepted(jax.random.fold_in(jax.random.fold_in(streams_of[10], part), 71), part),
        "down_map": gaussian(streams_of[8], (3, D, RANK), (3 * D) ** -0.5, 0.02734375, ((1, 8),)),
        "up_map": gaussian(streams_of[9], (RANK, D), (4 * D) ** -0.5, 0.0234375, ((1, 8),)),
    }


def attend_all(query_rows, cache_keys, cache_values, new_keys, new_values, valid):
    scaling = 1.0 / math.sqrt(HEAD_DIM)
    old_scores = jnp.einsum('rkgd,krld->rkgl', query_rows, cache_keys) * scaling
    old_scores = jnp.where(valid[:, None, None, :], old_scores, -jnp.inf)
    new_scores = jnp.einsum('rkgd,jkrd->rkgj', query_rows, new_keys) * scaling
    highest = jnp.maximum(lax.optimization_barrier(jnp.max(old_scores, axis=-1)), lax.optimization_barrier(jnp.max(new_scores, axis=-1)))
    old_weight = jnp.exp(old_scores - highest[..., None])
    new_weight = jnp.exp(new_scores - highest[..., None])
    totals = lax.optimization_barrier(jnp.sum(old_weight, axis=-1)) + lax.optimization_barrier(jnp.sum(new_weight, axis=-1))
    old_probs = (old_weight / totals[..., None]).astype(jnp.bfloat16).astype(jnp.float32)
    new_probs = (new_weight / totals[..., None]).astype(jnp.bfloat16).astype(jnp.float32)
    merged = jnp.einsum('rkgl,krld->rkgd', old_probs, cache_values)
    merged = merged + jnp.einsum('rkgj,jkrd->rkgd', new_probs, new_values)
    return merged.astype(jnp.bfloat16)

def reference(queries, cache, fresh_kv, lengths, w_out, residual, layers, accepted, down_map, up_map):
    group = HEADS // KV_HEADS
    cache_keys = cache[0].astype(jnp.float32)
    cache_values = cache[1].astype(jnp.float32)
    valid = jnp.arange(CACHE, dtype=jnp.int32)[None, :] < lengths[:, None]
    tops = []
    for decode_step in range(STEPS):
        query_rows = queries[decode_step].astype(jnp.float32).reshape(ROWS, KV_HEADS, group, HEAD_DIM)
        new_keys = fresh_kv[:decode_step + 1, 0].astype(jnp.float32)
        new_values = fresh_kv[:decode_step + 1, 1].astype(jnp.float32)
        attended = attend_all(query_rows, cache_keys, cache_values, new_keys, new_values, valid)
        attended = attended.reshape(ROWS, HEADS * HEAD_DIM)
        projected = jnp.dot(attended, w_out, preferred_element_type=jnp.float32)
        tops.append((residual[decode_step].astype(jnp.float32) + projected).astype(jnp.bfloat16))
    top_hidden = jnp.stack(tops)
    features = jnp.stack([layers[0, :-1], layers[1, :-1], top_hidden[:-1]], axis=2).astype(jnp.float32)
    target = top_hidden[1:].astype(jnp.float32)
    pre = jnp.einsum('srcj,cjk->srk', features, down_map.astype(jnp.float32))
    sigma = jax.nn.sigmoid(pre)
    gated = (pre * sigma).astype(jnp.bfloat16).astype(jnp.float32)
    pred = jnp.einsum('srk,kj->srj', gated, up_map.astype(jnp.float32))
    weight = accepted[:-1].astype(jnp.float32)
    cotangent = (weight[..., None] * (pred - target) / (STEPS - 1)).astype(jnp.bfloat16).astype(jnp.float32)
    grad_up = jnp.einsum('srk,srj->kj', gated, cotangent)
    back = jnp.einsum('srj,kj->srk', cotangent, up_map.astype(jnp.float32))
    dpre = (back * sigma * (1.0 + pre * (1.0 - sigma))).astype(jnp.bfloat16).astype(jnp.float32)
    grad_down = jnp.einsum('srcj,srk->cjk', features, dpre)
    return (top_hidden, grad_down.astype(jnp.bfloat16), grad_up.astype(jnp.bfloat16))
```

```python
import functools
import math

import jax
import jax.numpy as jnp
from jax import lax
from jax.experimental import pallas as pl
from jax.experimental.pallas import tpu as pltpu
from jax.sharding import PartitionSpec as P

MOST = 24
MESH = pl.DeviceIdType.MESH
BF16 = jnp.bfloat16
F32 = jnp.float32


def attend_kernel(group, q_ref, cache_ref, fresh_ref, bias_ref, out_ref):
    scaling = 1.0 / math.sqrt(q_ref.shape[-1])
    q = q_ref[:, 0]
    old = jnp.einsum("rqd,rld->rql", q, cache_ref[0, 0], preferred_element_type=F32)
    old = old * scaling + bias_ref[...]
    new = jnp.einsum("rqd,rjd->rqj", q, fresh_ref[0, 0], preferred_element_type=F32)
    step = lax.broadcasted_iota(jnp.int32, new.shape, 1) // group
    seen = lax.broadcasted_iota(jnp.int32, new.shape, 2) <= step
    new = jnp.where(seen, new * scaling, -jnp.inf)
    highest = jnp.maximum(
        jnp.max(old, axis=-1, keepdims=True), jnp.max(new, axis=-1, keepdims=True)
    )
    old = jnp.exp(old - highest)
    new = jnp.exp(new - highest)
    total = jnp.sum(old, axis=-1, keepdims=True) + jnp.sum(new, axis=-1, keepdims=True)
    share = 1.0 / total
    old = (old * share).astype(BF16)
    new = (new * share).astype(BF16)
    merged = jnp.einsum("rql,rld->rqd", old, cache_ref[1, 0], preferred_element_type=F32)
    merged += jnp.einsum("rqj,rjd->rqd", new, fresh_ref[1, 0], preferred_element_type=F32)
    out_ref[:, 0] = merged.astype(BF16)


def attend(queries, cache, fresh_kv, lengths):
    steps, rows, head_cols = queries.shape
    kv, span, dim = cache.shape[1], cache.shape[3], cache.shape[4]
    group = head_cols // dim // kv
    each = 8
    q = queries.reshape(steps, rows, kv, group, dim).transpose(1, 2, 0, 3, 4)
    q = q.reshape(rows, kv, steps * group, dim)
    fresh = fresh_kv.transpose(1, 2, 3, 0, 4)
    fresh = jnp.pad(fresh, ((0, 0), (0, 0), (0, 0), (0, 16 - steps), (0, 0)))
    held = jnp.arange(span, dtype=jnp.int32)[None, None, :] < lengths[:, None, None]
    bias = jnp.where(held, 0.0, -jnp.inf).astype(F32)
    out = pl.pallas_call(
        functools.partial(attend_kernel, group),
        grid=(kv, rows // each),
        in_specs=[
            pl.BlockSpec((each, 1, steps * group, dim), lambda k, i: (i, k, 0, 0)),
            pl.BlockSpec((2, 1, each, span, dim), lambda k, i: (0, k, i, 0, 0)),
            pl.BlockSpec((2, 1, each, 16, dim), lambda k, i: (0, k, i, 0, 0)),
            pl.BlockSpec((each, 1, span), lambda k, i: (i, 0, 0)),
        ],
        out_specs=pl.BlockSpec((each, 1, steps * group, dim), lambda k, i: (i, k, 0, 0)),
        out_shape=jax.ShapeDtypeStruct((rows, kv, steps * group, dim), BF16),
        compiler_params=pltpu.CompilerParams(vmem_limit_bytes=32 * 2**20),
        cost_estimate=pl.CostEstimate(
            flops=4 * rows * kv * steps * group * span * dim,
            bytes_accessed=2 * cache.size + 4 * queries.size,
            transcendentals=rows * kv * steps * group * span,
        ),
    )(q, cache, fresh, bias)
    out = out.reshape(rows, kv, steps, group, dim).transpose(2, 0, 1, 3, 4)
    return out.reshape(steps, rows, head_cols)


def project_kernel(
    n_t, n_dp, n_sec, att_ref, w_ref, res_ref, top_ref,
    held, w_vmem, acc, part, own, got,
    w_sem, local_sem, gs_sem, gr_sem, rs_sem, rr_sem,
):
    steps, rows, depth = att_ref.shape
    cols = w_ref.shape[1]
    blocks = n_dp * n_sec
    owned = res_ref.shape[1]
    halves, half = got.shape[1], got.shape[4]
    tile = 512
    t = lax.axis_index("tensor")
    me = lax.axis_index("dp") * n_sec + lax.axis_index("section")

    w_copies = [
        pltpu.make_async_copy(
            w_ref.at[:, pl.ds(h * half, half)], w_vmem.at[:, pl.ds(h * half, half)], w_sem.at[h]
        )
        for h in range(halves)
    ]
    locals_ = [
        pltpu.make_async_copy(att_ref.at[s], held.at[s, t], local_sem.at[s]) for s in range(steps)
    ]

    def other(k):
        return lax.rem(t + k, n_t)

    def peer(k):
        b = lax.rem(me + k, blocks)
        return b, {"dp": b // n_sec, "section": lax.rem(b, n_sec)}

    barrier = pltpu.get_barrier_semaphore()
    for k in range(1, n_t):
        pl.semaphore_signal(
            barrier, inc=1, device_id={"tensor": other(k)}, device_id_type=MESH
        )
    for k in range(1, blocks):
        pl.semaphore_signal(barrier, inc=1, device_id=peer(k)[1], device_id_type=MESH)
    pl.semaphore_wait(barrier, n_t - 1 + blocks - 1)

    def gather(s, k):
        return pltpu.make_async_remote_copy(
            src_ref=att_ref.at[s],
            dst_ref=held.at[s, t],
            send_sem=gs_sem.at[s, k - 1],
            recv_sem=gr_sem.at[s, k - 1],
            device_id={"tensor": other(k)},
            device_id_type=MESH,
        )

    def scatter(s, h, k):
        return pltpu.make_async_remote_copy(
            src_ref=part.at[s % 2, h, k - 1],
            dst_ref=got.at[s, h, k - 1],
            send_sem=rs_sem.at[s, h, k - 1],
            recv_sem=rr_sem.at[s, h, k - 1],
            device_id=peer(k)[1],
            device_id_type=MESH,
        )

    def start_gather(s):
        for k in range(n_t - 1, 0, -1):
            gather(s, k).start()

    def finish(s):
        for h in range(halves):
            for k in range(1, blocks):
                scatter(s, h, k).wait_recv()
            for c in range(0, half, tile):
                at = pl.ds(h * half + c, tile)
                total = own[s % 2, :, at] + res_ref[s, :, at].astype(F32)
                for k in range(1, blocks):
                    total += got[s, h, k - 1, :, pl.ds(c, tile)].astype(F32)
                top_ref[s, :, at] = total.astype(BF16)

    start_gather(0)
    for c in locals_:
        c.start()
    for c in w_copies:
        c.start()
    if steps > 1:
        start_gather(1)
    for c in locals_:
        c.wait()
    for s in range(steps):
        for k in range(1, n_t):
            gather(s, k).wait_recv()
        if s + 2 < steps:
            start_gather(s + 2)
        if s == 0:
            for c in w_copies:
                c.wait()
        if s >= 2:
            for h in range(halves):
                for k in range(1, blocks):
                    scatter(s - 2, h, k).wait_send()
        for h in range(halves):

            def body(i, _, s=s, h=h):
                at = pl.ds(pl.multiple_of(i * tile, tile), tile)
                wide = pl.ds(pl.multiple_of(h * half + i * tile, tile), tile)
                lhs = held[s].reshape(n_t * rows, depth)
                prod = jnp.dot(lhs, w_vmem[:, wide], preferred_element_type=F32)
                acc[...] = prod
                own[s % 2, :, wide] = acc[pl.ds(pl.multiple_of(me * owned, owned), owned), :]
                for k in range(1, blocks):
                    b = peer(k)[0]
                    part[s % 2, h, k - 1, :, at] = acc[
                        pl.ds(pl.multiple_of(b * owned, owned), owned), :
                    ].astype(BF16)
                return 0

            lax.fori_loop(0, half // tile, body, 0)
            for k in range(1, blocks):
                scatter(s, h, k).start()
        if s >= 1:
            finish(s - 1)
    finish(steps - 1)
    for s in range(max(0, steps - 2), steps):
        for h in range(halves):
            for k in range(1, blocks):
                scatter(s, h, k).wait_send()
    for s in range(steps):
        for k in range(1, n_t):
            gather(s, k).wait_send()


def project(mesh_shape, attended, w_out, residual):
    steps, rows, depth = attended.shape
    cols = w_out.shape[1]
    n_t, n_dp, n_sec = mesh_shape["tensor"], mesh_shape["dp"], mesh_shape["section"]
    blocks = n_dp * n_sec
    owned = residual.shape[1]
    if rows % 16 or owned % 16 or cols % 1024 or n_t < 2 or blocks < 2:
        whole = lax.all_gather(attended, "tensor", axis=1, tiled=True)
        partial_rows = jnp.einsum("srj,jk->srk", whole, w_out, preferred_element_type=F32)
        summed = lax.psum_scatter(
            partial_rows, ("dp", "section"), scatter_dimension=1, tiled=True
        )
        return (residual.astype(F32) + summed).astype(BF16)
    halves = 2
    half = cols // halves
    dma = pltpu.SemaphoreType.DMA
    return pl.pallas_call(
        functools.partial(project_kernel, n_t, n_dp, n_sec),
        out_shape=jax.ShapeDtypeStruct(residual.shape, BF16),
        in_specs=[
            pl.BlockSpec(memory_space=pl.ANY),
            pl.BlockSpec(memory_space=pl.ANY),
            pl.BlockSpec(memory_space=pltpu.VMEM),
        ],
        out_specs=pl.BlockSpec(memory_space=pltpu.VMEM),
        scratch_shapes=[
            pltpu.VMEM((steps, n_t, rows, depth), BF16),
            pltpu.VMEM((depth, cols), BF16),
            pltpu.VMEM((n_t * rows, 512), F32),
            pltpu.VMEM((2, halves, blocks - 1, owned, half), BF16),
            pltpu.VMEM((2, owned, cols), F32),
            pltpu.VMEM((steps, halves, blocks - 1, owned, half), BF16),
            dma((halves,)),
            dma((steps,)),
            dma((steps, n_t - 1)),
            dma((steps, n_t - 1)),
            dma((steps, halves, blocks - 1)),
            dma((steps, halves, blocks - 1)),
        ],
        compiler_params=pltpu.CompilerParams(
            collective_id=0, has_side_effects=True, vmem_limit_bytes=61 * 2**20
        ),
        cost_estimate=pl.CostEstimate(
            flops=2 * steps * rows * n_t * depth * cols,
            bytes_accessed=2 * w_out.size,
            transcendentals=0,
        ),
    )(attended, w_out, residual)


def on_device(
    mesh_shape, queries, cache, fresh_kv, lengths, w_out, residual, layers, accepted, down_map, up_map
):
    steps = queries.shape[0]
    n_t, n_dp, n_sec = mesh_shape["tensor"], mesh_shape["dp"], mesh_shape["section"]
    blocks = n_dp * n_sec
    owned = residual.shape[1]
    section = lax.axis_index("section")
    rank_width = up_map.shape[0]
    col_width = up_map.shape[1]

    most = min(MOST, owned)
    mine = lax.dynamic_slice_in_dim(accepted, section * owned, owned, axis=1)[: steps - 1]
    place = jnp.cumsum(mine, axis=1) - 1
    choose = (place[:, None, :] == jnp.arange(most)[None, :, None]) & (mine[:, None, :] > 0)
    choose = choose.astype(BF16)
    count = (steps - 1) * most

    def compact(x):
        picked = jnp.einsum("smr,srj->smj", choose, x, preferred_element_type=F32)
        return picked.astype(BF16).reshape(count, x.shape[-1])

    def swap(x, k):
        pairs = [(b, (b + k) % blocks) for b in range(blocks)]
        return lax.ppermute(x, ("dp", "section"), pairs)

    def half_for(x, k):
        b = (me + k) % blocks
        return lax.dynamic_slice_in_dim(x, (b % n_sec) * col_width, col_width, axis=x.ndim - 1)

    low_mid = jnp.stack([compact(layers[c, : steps - 1]) for c in range(2)])
    me = lax.axis_index("dp") * n_sec + section

    def in_order(pieces):
        axis = pieces[0].ndim - 2
        size = pieces[0].shape[axis]
        shape = list(pieces[0].shape)
        shape[axis] = blocks * size
        laid = jnp.zeros(shape, pieces[0].dtype)
        for k, piece in enumerate(pieces):
            b = (me + blocks - k) % blocks
            laid = lax.dynamic_update_slice_in_dim(laid, piece, b * size, axis=axis)
        return laid

    low_mid_all = in_order(
        [half_for(low_mid, 0)] + [swap(half_for(low_mid, k), k) for k in range(1, blocks)]
    )
    down_full = lax.all_gather(down_map, "section", axis=1, tiled=True)
    up_full = lax.all_gather(up_map, "section", axis=1, tiled=True)
    gram = lax.psum(
        jnp.einsum("kj,lj->kl", up_map, up_map, preferred_element_type=F32), ("tensor", "section")
    )
    pre_early = jnp.einsum("cnj,cjk->nk", low_mid, down_full[:2], preferred_element_type=F32)

    attended = attend(queries, cache, fresh_kv, lengths)
    top_hidden = project(mesh_shape, attended, w_out, residual)

    top = compact(top_hidden[: steps - 1])
    target = compact(top_hidden[1:])
    pair = jnp.stack([top, target])
    pair_all = in_order([half_for(pair, 0)] + [swap(half_for(pair, k), k) for k in range(1, blocks)])

    pre_part = pre_early + jnp.dot(top, down_full[2], preferred_element_type=F32)
    goal_part = jnp.einsum("nj,kj->nk", target, up_full, preferred_element_type=F32)
    both = jnp.concatenate([pre_part, goal_part], axis=1)
    if n_t <= 4:
        total = both
        for k in range(1, n_t):
            pairs = [(a, (a + k) % n_t) for a in range(n_t)]
            total = total + lax.ppermute(both, "tensor", pairs)
        both = total
    else:
        both = lax.psum(both, "tensor")
    pre, goal = both[:, :rank_width], both[:, rank_width:]
    sigma = jax.nn.sigmoid(pre)
    gated = (pre * sigma).astype(BF16)
    back = jnp.dot(gated.astype(F32), gram, precision=lax.Precision.HIGHEST) - goal
    back = back / (steps - 1)
    dpre = (back * sigma * (1.0 + pre * (1.0 - sigma))).astype(BF16)
    inner = jnp.concatenate([gated, dpre], axis=1)
    inner_all = in_order([inner] + [swap(inner, k) for k in range(1, blocks)])
    gated, dpre = inner_all[:, :rank_width], inner_all[:, rank_width:]

    pred = jnp.dot(gated, up_map, preferred_element_type=F32)
    cotangent = ((pred - pair_all[1].astype(F32)) / (steps - 1)).astype(BF16)
    grad_up = jnp.einsum("nk,nj->kj", gated, cotangent, preferred_element_type=F32).astype(BF16)
    grad_down = jnp.stack(
        [
            jnp.einsum("nj,nk->jk", x, dpre, preferred_element_type=F32).astype(BF16)
            for x in (low_mid_all[0], low_mid_all[1], pair_all[0])
        ]
    )
    return top_hidden, grad_down, grad_up


def solution(mesh):
    placed = (
        P("groups", "tensor", ("dp", "section")),
        P("groups", ("dp", "section"), "tensor", None, None),
        P("groups", None, ("dp", "section"), "tensor", None),
        P(("groups", "tensor")),
        P(("dp", "section"), "tensor"),
        P("groups", ("dp", "section"), "tensor"),
        P("groups", None, ("dp", "section"), "tensor"),
        P("groups", "dp"),
        P(None, ("tensor", "section"), None),
        P(None, ("tensor", "section")),
    )
    return jax.shard_map(
        functools.partial(on_device, dict(mesh.shape)),
        mesh=mesh,
        in_specs=placed,
        out_specs=(
            P("groups", ("dp", "section"), "tensor"),
            P("groups", ("tensor", "section"), None),
            P("groups", ("tensor", "section")),
        ),
        check_vma=False,
    )
```

```python
import functools
import math

import jax
import jax.numpy as jnp
from jax import lax
from jax.experimental import pallas as pl
from jax.experimental.pallas import tpu as pltpu
from jax.sharding import PartitionSpec as P

MOST = 24
MESH = pl.DeviceIdType.MESH
BF16 = jnp.bfloat16
F32 = jnp.float32


def attend_kernel(group, q_ref, cache_ref, fresh_ref, bias_ref, out_ref):
    scaling = 1.0 / math.sqrt(q_ref.shape[-1])
    q = q_ref[:, 0]
    old = jnp.einsum("rqd,rld->rql", q, cache_ref[0, 0], preferred_element_type=F32)
    old = old * scaling + bias_ref[...]
    new = jnp.einsum("rqd,rjd->rqj", q, fresh_ref[0, 0], preferred_element_type=F32)
    step = lax.broadcasted_iota(jnp.int32, new.shape, 1) // group
    seen = lax.broadcasted_iota(jnp.int32, new.shape, 2) <= step
    new = jnp.where(seen, new * scaling, -jnp.inf)
    highest = jnp.maximum(
        jnp.max(old, axis=-1, keepdims=True), jnp.max(new, axis=-1, keepdims=True)
    )
    old = jnp.exp(old - highest)
    new = jnp.exp(new - highest)
    total = jnp.sum(old, axis=-1, keepdims=True) + jnp.sum(new, axis=-1, keepdims=True)
    share = 1.0 / total
    old = (old * share).astype(BF16)
    new = (new * share).astype(BF16)
    merged = jnp.einsum("rql,rld->rqd", old, cache_ref[1, 0], preferred_element_type=F32)
    merged += jnp.einsum("rqj,rjd->rqd", new, fresh_ref[1, 0], preferred_element_type=F32)
    out_ref[:, 0] = merged.astype(BF16)


def attend(queries, cache, fresh_kv, lengths):
    steps, rows, head_cols = queries.shape
    kv, span, dim = cache.shape[1], cache.shape[3], cache.shape[4]
    group = head_cols // dim // kv
    each = 8
    q = queries.reshape(steps, rows, kv, group, dim).transpose(1, 2, 0, 3, 4)
    q = q.reshape(rows, kv, steps * group, dim)
    fresh = fresh_kv.transpose(1, 2, 3, 0, 4)
    fresh = jnp.pad(fresh, ((0, 0), (0, 0), (0, 0), (0, 16 - steps), (0, 0)))
    held = jnp.arange(span, dtype=jnp.int32)[None, None, :] < lengths[:, None, None]
    bias = jnp.where(held, 0.0, -jnp.inf).astype(F32)
    out = pl.pallas_call(
        functools.partial(attend_kernel, group),
        grid=(kv, rows // each),
        in_specs=[
            pl.BlockSpec((each, 1, steps * group, dim), lambda k, i: (i, k, 0, 0)),
            pl.BlockSpec((2, 1, each, span, dim), lambda k, i: (0, k, i, 0, 0)),
            pl.BlockSpec((2, 1, each, 16, dim), lambda k, i: (0, k, i, 0, 0)),
            pl.BlockSpec((each, 1, span), lambda k, i: (i, 0, 0)),
        ],
        out_specs=pl.BlockSpec((each, 1, steps * group, dim), lambda k, i: (i, k, 0, 0)),
        out_shape=jax.ShapeDtypeStruct((rows, kv, steps * group, dim), BF16),
        compiler_params=pltpu.CompilerParams(vmem_limit_bytes=32 * 2**20),
        cost_estimate=pl.CostEstimate(
            flops=4 * rows * kv * steps * group * span * dim,
            bytes_accessed=2 * cache.size + 4 * queries.size,
            transcendentals=rows * kv * steps * group * span,
        ),
    )(q, cache, fresh, bias)
    out = out.reshape(rows, kv, steps, group, dim).transpose(2, 0, 1, 3, 4)
    return out.reshape(steps, rows, head_cols)


def project_kernel(
    n_t, n_dp, n_sec, att_ref, w_ref, res_ref, choose_ref, lm_ref, gram_ref,
    top_ref, pair_ref, lm_all, pair_all, gram_all,
    held, w_vmem, acc, part, own, got,
    w_sem, local_sem, gs_sem, gr_sem, rs_sem, rr_sem,
    lms_sem, lmr_sem, ps_sem, pr_sem, grs_sem, grr_sem, keep_sem,
):
    steps, rows, depth = att_ref.shape
    cols = w_ref.shape[1]
    blocks = n_dp * n_sec
    owned = res_ref.shape[1]
    halves, half = got.shape[1], got.shape[4]
    tile = 512
    t = lax.axis_index("tensor")
    me = lax.axis_index("dp") * n_sec + lax.axis_index("section")

    w_copies = [
        pltpu.make_async_copy(
            w_ref.at[:, pl.ds(h * half, half)], w_vmem.at[:, pl.ds(h * half, half)], w_sem.at[h]
        )
        for h in range(halves)
    ]
    locals_ = [
        pltpu.make_async_copy(att_ref.at[s], held.at[s, t], local_sem.at[s]) for s in range(steps)
    ]

    def other(k):
        return lax.rem(t + k, n_t)

    def peer(k):
        b = lax.rem(me + k, blocks)
        return b, {"dp": b // n_sec, "section": lax.rem(b, n_sec)}

    barrier = pltpu.get_barrier_semaphore()
    for k in range(1, n_t):
        pl.semaphore_signal(
            barrier, inc=1, device_id={"tensor": other(k)}, device_id_type=MESH
        )
    for k in range(1, blocks):
        pl.semaphore_signal(barrier, inc=1, device_id=peer(k)[1], device_id_type=MESH)
    pl.semaphore_wait(barrier, n_t - 1 + blocks - 1)

    def sends(way, j):
        return (t >= j) & (t < n_t - 1) if way == 0 else (t + j < n_t) & (t > 0)

    def receives(way, j):
        return t - 1 - j >= 0 if way == 0 else t + 1 + j < n_t

    def gather(s, way, j):
        block = lax.rem(t - j + n_t, n_t) if way == 0 else lax.rem(t + j, n_t)
        to = lax.rem(t + 1, n_t) if way == 0 else lax.rem(t + n_t - 1, n_t)
        return pltpu.make_async_remote_copy(
            src_ref=att_ref.at[s] if j == 0 else held.at[s, block],
            dst_ref=held.at[s, block],
            send_sem=gs_sem.at[s, way, j],
            recv_sem=gr_sem.at[s, way, j],
            device_id={"tensor": to},
            device_id_type=MESH,
        )

    def pass_on(s):
        for j in range(n_t - 1):
            for way in range(2):

                @pl.when(receives(way, j))
                def _(s=s, way=way, j=j):
                    gather(s, way, j).wait_recv()

                if j + 1 < n_t - 1:

                    @pl.when(sends(way, j + 1))
                    def _(s=s, way=way, j=j):
                        gather(s, way, j + 1).start()

    width = lm_all.shape[-1]
    chosen = choose_ref.shape[1]

    def columns(b):
        return pl.ds(pl.multiple_of(lax.rem(b, n_sec) * width, width), width)

    def send_lm(k):
        b, to = peer(k)
        return pltpu.make_async_remote_copy(
            src_ref=lm_ref.at[:, :, columns(b)], dst_ref=lm_all.at[me],
            send_sem=lms_sem.at[k - 1], recv_sem=lmr_sem.at[k - 1],
            device_id=to, device_id_type=MESH,
        )

    def send_pair(a, s, k):
        b, to = peer(k)
        at = pl.ds(s * chosen, chosen)
        return pltpu.make_async_remote_copy(
            src_ref=pair_ref.at[a, at, columns(b)], dst_ref=pair_all.at[me, a, at],
            send_sem=ps_sem.at[a, s, k - 1], recv_sem=pr_sem.at[a, s, k - 1],
            device_id=to, device_id_type=MESH,
        )

    def send_gram(k):
        return pltpu.make_async_remote_copy(
            src_ref=gram_ref, dst_ref=gram_all.at[t],
            send_sem=grs_sem.at[k - 1], recv_sem=grr_sem.at[k - 1],
            device_id={"tensor": other(k)}, device_id_type=MESH,
        )

    def scatter(s, h, k):
        return pltpu.make_async_remote_copy(
            src_ref=part.at[s % 2, h, k - 1],
            dst_ref=got.at[s, h, k - 1],
            send_sem=rs_sem.at[s, h, k - 1],
            recv_sem=rr_sem.at[s, h, k - 1],
            device_id=peer(k)[1],
            device_id_type=MESH,
        )

    def start_gather(s):
        for way in range(2):

            @pl.when(sends(way, 0))
            def _(s=s, way=way):
                gather(s, way, 0).start()

    def finish(s):
        for h in range(halves):
            for k in range(1, blocks):
                scatter(s, h, k).wait_recv()
            for c in range(0, half, tile):
                at = pl.ds(h * half + c, tile)
                total = own[s % 2, :, at] + res_ref[s, :, at].astype(F32)
                for k in range(1, blocks):
                    total += got[s, h, k - 1, :, pl.ds(c, tile)].astype(F32)
                total = total.astype(BF16)
                top_ref[s, :, at] = total
                for a, at_step in ((0, s), (1, s - 1)):
                    if 0 <= at_step < steps - 1:
                        picked = jnp.dot(choose_ref[at_step], total, preferred_element_type=F32)
                        pair_ref[a, pl.ds(at_step * chosen, chosen), at] = picked.astype(BF16)
        for a, at_step in ((0, s), (1, s - 1)):
            if 0 <= at_step < steps - 1:
                for k in range(1, blocks):
                    send_pair(a, at_step, k).start()

    start_gather(0)
    for c in locals_:
        c.start()
    for c in w_copies:
        c.start()
    if steps > 1:
        start_gather(1)
    for k in range(1, blocks):
        send_lm(k).start()
    for k in range(1, n_t):
        send_gram(k).start()
    keeps = [
        pltpu.make_async_copy(lm_ref.at[:, :, columns(me)], lm_all.at[me], keep_sem.at[0]),
        pltpu.make_async_copy(gram_ref, gram_all.at[t], keep_sem.at[1]),
    ]
    for c in keeps:
        c.start()
    for c in locals_:
        c.wait()
    for s in range(steps):
        pass_on(s)
        if s + 2 < steps:
            start_gather(s + 2)
        if s == 0:
            for c in w_copies:
                c.wait()
        if s >= 2:
            for h in range(halves):
                for k in range(1, blocks):
                    scatter(s - 2, h, k).wait_send()
        for h in range(halves):

            def body(i, _, s=s, h=h):
                at = pl.ds(pl.multiple_of(i * tile, tile), tile)
                wide = pl.ds(pl.multiple_of(h * half + i * tile, tile), tile)
                lhs = held[s].reshape(n_t * rows, depth)
                prod = jnp.dot(lhs, w_vmem[:, wide], preferred_element_type=F32)
                acc[...] = prod
                own[s % 2, :, wide] = acc[pl.ds(pl.multiple_of(me * owned, owned), owned), :]
                for k in range(1, blocks):
                    b = peer(k)[0]
                    part[s % 2, h, k - 1, :, at] = acc[
                        pl.ds(pl.multiple_of(b * owned, owned), owned), :
                    ].astype(BF16)
                return 0

            lax.fori_loop(0, half // tile, body, 0)
            for k in range(1, blocks):
                scatter(s, h, k).start()
        if s >= 1:
            finish(s - 1)
    finish(steps - 1)
    for s in range(max(0, steps - 2), steps):
        for h in range(halves):
            for k in range(1, blocks):
                scatter(s, h, k).wait_send()
    last = pltpu.make_async_copy(pair_ref.at[:, :, columns(me)], pair_all.at[me], keep_sem.at[2])
    last.start()
    for s in range(steps):
        for way in range(2):
            for j in range(n_t - 1):

                @pl.when(sends(way, j))
                def _(s=s, way=way, j=j):
                    gather(s, way, j).wait_send()

    for k in range(1, blocks):
        send_lm(k).wait()
    for k in range(1, n_t):
        send_gram(k).wait()
    for s in range(steps - 1):
        for a in range(2):
            for k in range(1, blocks):
                send_pair(a, s, k).wait()
    for c in keeps + [last]:
        c.wait()


def train_kernel(
    n_t, n_dp, n_sec, scale, pair_ref, lm_ref, down_ref, up_all, up_ref, gram_all, lm_all, pair_all,
    grad_down_ref, grad_up_ref,
    down, ups, gsum, gram_got, both, both_all, inner, inner_all, lms, pairs,
    in_sem, gs_sem, gr_sem, bs_sem, br_sem, is_sem, ir_sem,
):
    blocks = n_dp * n_sec
    count = pair_ref.shape[1]
    rank_width = up_ref.shape[0]
    width = up_ref.shape[1]
    t = lax.axis_index("tensor")
    section = lax.axis_index("section")
    me = lax.axis_index("dp") * n_sec + section

    loads = [
        pltpu.make_async_copy(up_all, ups, in_sem.at[0]),
        pltpu.make_async_copy(down_ref, down, in_sem.at[1]),
        pltpu.make_async_copy(lm_all, lms, in_sem.at[2]),
        pltpu.make_async_copy(pair_all, pairs, in_sem.at[3]),
    ]
    for c in loads:
        c.start()

    def peer(k):
        b = lax.rem(me + k, blocks)
        return {"dp": b // n_sec, "section": lax.rem(b, n_sec)}

    barrier = pltpu.get_barrier_semaphore()
    for k in range(1, n_t):
        pl.semaphore_signal(
            barrier, inc=1, device_id={"tensor": lax.rem(t + k, n_t)}, device_id_type=MESH
        )
    for k in range(1, blocks):
        pl.semaphore_signal(barrier, inc=1, device_id=peer(k), device_id_type=MESH)
    pl.semaphore_wait(barrier, n_t - 1 + blocks - 1)

    def send_gram(k):
        return pltpu.make_async_remote_copy(
            src_ref=gsum, dst_ref=gram_got.at[section],
            send_sem=gs_sem.at[k - 1], recv_sem=gr_sem.at[k - 1],
            device_id={"section": lax.rem(section + k, n_sec)}, device_id_type=MESH,
        )

    def send_both(k):
        return pltpu.make_async_remote_copy(
            src_ref=both, dst_ref=both_all.at[t],
            send_sem=bs_sem.at[k - 1], recv_sem=br_sem.at[k - 1],
            device_id={"tensor": lax.rem(t + k, n_t)}, device_id_type=MESH,
        )

    def send_inner(k):
        return pltpu.make_async_remote_copy(
            src_ref=inner, dst_ref=inner_all.at[me],
            send_sem=is_sem.at[k - 1], recv_sem=ir_sem.at[k - 1],
            device_id=peer(k), device_id_type=MESH,
        )

    gsum[...] = sum(gram_all[i] for i in range(n_t))
    gram_got[section] = gsum[...]
    for k in range(1, n_sec):
        send_gram(k).start()
    loads[0].wait()
    both[:, rank_width:] = lax.dot_general(
        pair_ref[1], ups[...], (((1,), (1,)), ((), ())), preferred_element_type=F32
    )
    loads[1].wait()
    pre = jnp.dot(pair_ref[0], down[2], preferred_element_type=F32)
    for c in range(2):
        pre += jnp.dot(lm_ref[c], down[c], preferred_element_type=F32)
    both[:, :rank_width] = pre
    both_all[t] = both[...]
    for k in range(1, n_t):
        send_both(k).start()
    for k in range(1, n_sec):
        send_gram(k).wait()
    for k in range(1, n_t):
        send_both(k).wait()
    total = both_all[0]
    for i in range(1, n_t):
        total += both_all[i]
    gram = gram_got[0]
    for i in range(1, n_sec):
        gram += gram_got[i]
    pre, goal = total[:, :rank_width], total[:, rank_width:]
    sigma = jax.nn.sigmoid(pre)
    gated = (pre * sigma).astype(BF16)
    back = jnp.dot(
        gated.astype(F32), gram, precision=lax.Precision.HIGHEST, preferred_element_type=F32
    ) - goal
    back = back / scale
    inner[:, :rank_width] = gated
    inner[:, rank_width:] = (back * sigma * (1.0 + pre * (1.0 - sigma))).astype(BF16)
    inner_all[me] = inner[...]
    for k in range(1, blocks):
        send_inner(k).start()
    loads[2].wait()
    loads[3].wait()
    for k in range(1, blocks):
        send_inner(k).wait()
    rows = blocks * count
    gated = inner_all[:, :, :rank_width].reshape(rows, rank_width)
    dpre = inner_all[:, :, rank_width:].reshape(rows, rank_width)
    tile = min(512, width)

    def body(i, _):
        at = pl.ds(pl.multiple_of(i * tile, tile), tile)
        over = (((0,), (0,)), ((), ()))
        pred = jnp.dot(gated, up_ref[:, at], preferred_element_type=F32)
        target = pairs[:, 1, :, at].reshape(rows, tile).astype(F32)
        cotangent = ((pred - target) / scale).astype(BF16)
        grad_up_ref[:, at] = lax.dot_general(
            gated, cotangent, over, preferred_element_type=F32
        ).astype(BF16)
        for c in range(3):
            x = lms[:, c, :, at] if c < 2 else pairs[:, 0, :, at]
            grad_down_ref[c, at, :] = lax.dot_general(
                x.reshape(rows, tile), dpre, over, preferred_element_type=F32
            ).astype(BF16)
        return 0

    lax.fori_loop(0, width // tile, body, 0)


def fits(mesh_shape, attended, w_out, residual):
    blocks = mesh_shape["dp"] * mesh_shape["section"]
    whole = attended.shape[1] % 16 == 0 and residual.shape[1] % 32 == 0
    return whole and w_out.shape[1] % 1024 == 0 and mesh_shape["tensor"] > 1 and blocks > 1


def project_plain(attended, w_out, residual):
    whole = lax.all_gather(attended, "tensor", axis=1, tiled=True)
    partial_rows = jnp.einsum("srj,jk->srk", whole, w_out, preferred_element_type=F32)
    summed = lax.psum_scatter(partial_rows, ("dp", "section"), scatter_dimension=1, tiled=True)
    return (residual.astype(F32) + summed).astype(BF16)


def project(mesh_shape, attended, w_out, residual, choose, low_mid, gram):
    steps, rows, depth = attended.shape
    cols = w_out.shape[1]
    n_t, n_dp, n_sec = mesh_shape["tensor"], mesh_shape["dp"], mesh_shape["section"]
    blocks = n_dp * n_sec
    owned = residual.shape[1]
    count = low_mid.shape[1]
    halves = 2
    half = cols // halves
    dma = pltpu.SemaphoreType.DMA
    hbm, vmem = pl.BlockSpec(memory_space=pl.ANY), pl.BlockSpec(memory_space=pltpu.VMEM)
    spread = jax.ShapeDtypeStruct((blocks, 2, count, cols // n_sec), BF16)
    return pl.pallas_call(
        functools.partial(project_kernel, n_t, n_dp, n_sec),
        out_shape=(
            jax.ShapeDtypeStruct(residual.shape, BF16),
            jax.ShapeDtypeStruct((2, count, cols), BF16),
            spread,
            spread,
            jax.ShapeDtypeStruct((n_t,) + gram.shape, F32),
        ),
        in_specs=[hbm, hbm, vmem, vmem, hbm, hbm],
        out_specs=(vmem, vmem, hbm, hbm, hbm),
        scratch_shapes=[
            pltpu.VMEM((steps, n_t, rows, depth), BF16),
            pltpu.VMEM((depth, cols), BF16),
            pltpu.VMEM((n_t * rows, 512), F32),
            pltpu.VMEM((2, halves, blocks - 1, owned, half), BF16),
            pltpu.VMEM((2, owned, cols), F32),
            pltpu.VMEM((steps, halves, blocks - 1, owned, half), BF16),
            dma((halves,)),
            dma((steps,)),
            dma((steps, 2, n_t - 1)),
            dma((steps, 2, n_t - 1)),
            dma((steps, halves, blocks - 1)),
            dma((steps, halves, blocks - 1)),
            dma((blocks - 1,)),
            dma((blocks - 1,)),
            dma((2, steps - 1, blocks - 1)),
            dma((2, steps - 1, blocks - 1)),
            dma((n_t - 1,)),
            dma((n_t - 1,)),
            dma((3,)),
        ],
        compiler_params=pltpu.CompilerParams(
            collective_id=0, has_side_effects=True, vmem_limit_bytes=62 * 2**20
        ),
        cost_estimate=pl.CostEstimate(
            flops=2 * steps * rows * n_t * depth * cols,
            bytes_accessed=2 * w_out.size,
            transcendentals=0,
        ),
    )(attended, w_out, residual, choose, low_mid, gram)


def train(mesh_shape, scale, pair, low_mid, down_full, up_full, up_map, gram_all, lm_all, pair_all):
    n_t, n_dp, n_sec = mesh_shape["tensor"], mesh_shape["dp"], mesh_shape["section"]
    blocks = n_dp * n_sec
    count = pair.shape[1]
    rank_width, width = up_map.shape
    dma = pltpu.SemaphoreType.DMA
    hbm, vmem = pl.BlockSpec(memory_space=pl.ANY), pl.BlockSpec(memory_space=pltpu.VMEM)
    square = (rank_width, rank_width)
    return pl.pallas_call(
        functools.partial(train_kernel, n_t, n_dp, n_sec, scale),
        out_shape=(
            jax.ShapeDtypeStruct((3, width, rank_width), BF16),
            jax.ShapeDtypeStruct((rank_width, width), BF16),
        ),
        in_specs=[vmem, vmem, hbm, hbm, vmem, vmem, hbm, hbm],
        out_specs=(vmem, vmem),
        scratch_shapes=[
            pltpu.VMEM(down_full.shape, BF16),
            pltpu.VMEM(up_full.shape, BF16),
            pltpu.VMEM(square, F32),
            pltpu.VMEM((n_sec,) + square, F32),
            pltpu.VMEM((count, 2 * rank_width), F32),
            pltpu.VMEM((n_t, count, 2 * rank_width), F32),
            pltpu.VMEM((count, 2 * rank_width), BF16),
            pltpu.VMEM((blocks, count, 2 * rank_width), BF16),
            pltpu.VMEM(lm_all.shape, BF16),
            pltpu.VMEM(pair_all.shape, BF16),
            dma((4,)),
            dma((max(1, n_sec - 1),)),
            dma((max(1, n_sec - 1),)),
            dma((n_t - 1,)),
            dma((n_t - 1,)),
            dma((blocks - 1,)),
            dma((blocks - 1,)),
        ],
        compiler_params=pltpu.CompilerParams(
            collective_id=1, has_side_effects=True, vmem_limit_bytes=48 * 2**20
        ),
    )(pair, low_mid, down_full, up_full, up_map, gram_all, lm_all, pair_all)


def on_device(
    mesh_shape, queries, cache, fresh_kv, lengths, w_out, residual, layers, accepted, down_map, up_map
):
    steps = queries.shape[0]
    n_t, n_dp, n_sec = mesh_shape["tensor"], mesh_shape["dp"], mesh_shape["section"]
    blocks = n_dp * n_sec
    owned = residual.shape[1]
    section = lax.axis_index("section")
    rank_width = up_map.shape[0]
    col_width = up_map.shape[1]

    kernels = fits(mesh_shape, queries, w_out, residual)
    most = 32 if kernels else min(MOST, owned)
    mine = lax.dynamic_slice_in_dim(accepted, section * owned, owned, axis=1)[: steps - 1]
    place = jnp.cumsum(mine, axis=1) - 1
    choose = (place[:, None, :] == jnp.arange(most)[None, :, None]) & (mine[:, None, :] > 0)
    choose = choose.astype(BF16)
    count = (steps - 1) * most

    def compact(x):
        picked = jnp.einsum("smr,srj->smj", choose, x, preferred_element_type=F32)
        return picked.astype(BF16).reshape(count, x.shape[-1])

    def swap(x, k):
        pairs = [(b, (b + k) % blocks) for b in range(blocks)]
        return lax.ppermute(x, ("dp", "section"), pairs)

    def half_for(x, k):
        b = (me + k) % blocks
        return lax.dynamic_slice_in_dim(x, (b % n_sec) * col_width, col_width, axis=x.ndim - 1)

    low_mid = jnp.stack([compact(layers[c, : steps - 1]) for c in range(2)])
    me = lax.axis_index("dp") * n_sec + section

    def in_order(pieces):
        axis = pieces[0].ndim - 2
        size = pieces[0].shape[axis]
        shape = list(pieces[0].shape)
        shape[axis] = blocks * size
        laid = jnp.zeros(shape, pieces[0].dtype)
        for k, piece in enumerate(pieces):
            b = (me + blocks - k) % blocks
            laid = lax.dynamic_update_slice_in_dim(laid, piece, b * size, axis=axis)
        return laid

    down_full = lax.all_gather(down_map, "section", axis=1, tiled=True)
    up_full = lax.all_gather(up_map, "section", axis=1, tiled=True)
    gram = jnp.einsum("kj,lj->kl", up_map, up_map, preferred_element_type=F32)
    attended = attend(queries, cache, fresh_kv, lengths)
    if kernels:
        top_hidden, pair, lm_all, pair_all, gram_all = project(
            mesh_shape, attended, w_out, residual, choose, low_mid, gram
        )
        grad_down, grad_up = train(
            mesh_shape, steps - 1, pair, low_mid, down_full, up_full, up_map,
            gram_all, lm_all, pair_all,
        )
        return top_hidden, grad_down, grad_up

    low_mid_all = in_order(
        [half_for(low_mid, 0)] + [swap(half_for(low_mid, k), k) for k in range(1, blocks)]
    )
    gram = lax.psum(gram, ("tensor", "section"))
    pre_early = jnp.einsum("cnj,cjk->nk", low_mid, down_full[:2], preferred_element_type=F32)

    top_hidden = project_plain(attended, w_out, residual)

    top = compact(top_hidden[: steps - 1])
    target = compact(top_hidden[1:])
    pair = jnp.stack([top, target])
    pair_all = in_order([half_for(pair, 0)] + [swap(half_for(pair, k), k) for k in range(1, blocks)])

    pre_part = pre_early + jnp.dot(top, down_full[2], preferred_element_type=F32)
    goal_part = jnp.einsum("nj,kj->nk", target, up_full, preferred_element_type=F32)
    both = jnp.concatenate([pre_part, goal_part], axis=1)
    if n_t <= 4:
        total = both
        for k in range(1, n_t):
            pairs = [(a, (a + k) % n_t) for a in range(n_t)]
            total = total + lax.ppermute(both, "tensor", pairs)
        both = total
    else:
        both = lax.psum(both, "tensor")
    pre, goal = both[:, :rank_width], both[:, rank_width:]
    sigma = jax.nn.sigmoid(pre)
    gated = (pre * sigma).astype(BF16)
    back = jnp.dot(gated.astype(F32), gram, precision=lax.Precision.HIGHEST) - goal
    back = back / (steps - 1)
    dpre = (back * sigma * (1.0 + pre * (1.0 - sigma))).astype(BF16)
    inner = jnp.concatenate([gated, dpre], axis=1)
    inner_all = in_order([inner] + [swap(inner, k) for k in range(1, blocks)])
    gated, dpre = inner_all[:, :rank_width], inner_all[:, rank_width:]

    pred = jnp.dot(gated, up_map, preferred_element_type=F32)
    cotangent = ((pred - pair_all[1].astype(F32)) / (steps - 1)).astype(BF16)
    grad_up = jnp.einsum("nk,nj->kj", gated, cotangent, preferred_element_type=F32).astype(BF16)
    grad_down = jnp.stack(
        [
            jnp.einsum("nj,nk->jk", x, dpre, preferred_element_type=F32).astype(BF16)
            for x in (low_mid_all[0], low_mid_all[1], pair_all[0])
        ]
    )
    return top_hidden, grad_down, grad_up


def solution(mesh):
    placed = (
        P("groups", "tensor", ("dp", "section")),
        P("groups", ("dp", "section"), "tensor", None, None),
        P("groups", None, ("dp", "section"), "tensor", None),
        P(("groups", "tensor")),
        P(("dp", "section"), "tensor"),
        P("groups", ("dp", "section"), "tensor"),
        P("groups", None, ("dp", "section"), "tensor"),
        P("groups", "dp"),
        P(None, ("tensor", "section"), None),
        P(None, ("tensor", "section")),
    )
    return jax.shard_map(
        functools.partial(on_device, dict(mesh.shape)),
        mesh=mesh,
        in_specs=placed,
        out_specs=(
            P("groups", ("dp", "section"), "tensor"),
            P("groups", ("tensor", "section"), None),
            P("groups", ("tensor", "section")),
        ),
        check_vma=False,
    )
```

```python
import functools
import math

import jax
import jax.numpy as jnp
from jax import lax
from jax.experimental import pallas as pl
from jax.experimental.pallas import tpu as pltpu
from jax.sharding import PartitionSpec as P

MOST = 24
MESH = pl.DeviceIdType.MESH
BF16 = jnp.bfloat16
F32 = jnp.float32


def attend_kernel(group, q_ref, cache_ref, fresh_ref, bias_ref, out_ref):
    scaling = 1.0 / math.sqrt(q_ref.shape[-1])
    q = q_ref[:, 0]
    old = jnp.einsum("rqd,rld->rql", q, cache_ref[0, 0], preferred_element_type=F32)
    old = old * scaling + bias_ref[...]
    new = jnp.einsum("rqd,rjd->rqj", q, fresh_ref[0, 0], preferred_element_type=F32)
    step = lax.broadcasted_iota(jnp.int32, new.shape, 1) // group
    seen = lax.broadcasted_iota(jnp.int32, new.shape, 2) <= step
    new = jnp.where(seen, new * scaling, -jnp.inf)
    highest = jnp.maximum(
        jnp.max(old, axis=-1, keepdims=True), jnp.max(new, axis=-1, keepdims=True)
    )
    old = jnp.exp(old - highest)
    new = jnp.exp(new - highest)
    total = jnp.sum(old, axis=-1, keepdims=True) + jnp.sum(new, axis=-1, keepdims=True)
    share = 1.0 / total
    old = (old * share).astype(BF16)
    new = (new * share).astype(BF16)
    merged = jnp.einsum("rql,rld->rqd", old, cache_ref[1, 0], preferred_element_type=F32)
    merged += jnp.einsum("rqj,rjd->rqd", new, fresh_ref[1, 0], preferred_element_type=F32)
    out_ref[:, 0] = merged.astype(BF16)


def attend(queries, cache, fresh_kv, lengths):
    steps, rows, head_cols = queries.shape
    kv, span, dim = cache.shape[1], cache.shape[3], cache.shape[4]
    group = head_cols // dim // kv
    each = 8
    q = queries.reshape(steps, rows, kv, group, dim).transpose(1, 2, 0, 3, 4)
    q = q.reshape(rows, kv, steps * group, dim)
    fresh = fresh_kv.transpose(1, 2, 3, 0, 4)
    fresh = jnp.pad(fresh, ((0, 0), (0, 0), (0, 0), (0, 16 - steps), (0, 0)))
    held = jnp.arange(span, dtype=jnp.int32)[None, None, :] < lengths[:, None, None]
    bias = jnp.where(held, 0.0, -jnp.inf).astype(F32)
    out = pl.pallas_call(
        functools.partial(attend_kernel, group),
        grid=(kv, rows // each),
        in_specs=[
            pl.BlockSpec((each, 1, steps * group, dim), lambda k, i: (i, k, 0, 0)),
            pl.BlockSpec((2, 1, each, span, dim), lambda k, i: (0, k, i, 0, 0)),
            pl.BlockSpec((2, 1, each, 16, dim), lambda k, i: (0, k, i, 0, 0)),
            pl.BlockSpec((each, 1, span), lambda k, i: (i, 0, 0)),
        ],
        out_specs=pl.BlockSpec((each, 1, steps * group, dim), lambda k, i: (i, k, 0, 0)),
        out_shape=jax.ShapeDtypeStruct((rows, kv, steps * group, dim), BF16),
        compiler_params=pltpu.CompilerParams(vmem_limit_bytes=32 * 2**20),
        cost_estimate=pl.CostEstimate(
            flops=4 * rows * kv * steps * group * span * dim,
            bytes_accessed=2 * cache.size + 4 * queries.size,
            transcendentals=rows * kv * steps * group * span,
        ),
    )(q, cache, fresh, bias)
    out = out.reshape(rows, kv, steps, group, dim).transpose(2, 0, 1, 3, 4)
    return out.reshape(steps, rows, head_cols)


def project_kernel(
    n_t, n_dp, n_sec, att_ref, w_ref, res_ref, choose_ref, lm_ref,
    top_ref, pair_ref, lm_all, pair_all,
    held, w_vmem, acc, part, own, got, part_dp, got_dp,
    w_sem, local_sem, gs_sem, gr_sem, rs_sem, rr_sem, ds_sem, dr_sem,
    lms_sem, lmr_sem, ps_sem, pr_sem, keep_sem,
):
    steps, rows, depth = att_ref.shape
    cols = w_ref.shape[1]
    blocks = n_dp * n_sec
    owned = res_ref.shape[1]
    halves, half = got.shape[1], got.shape[5]
    tile = 512
    ahead = 3
    pieces = gs_sem.shape[3]
    t = lax.axis_index("tensor")
    d, sec = lax.axis_index("dp"), lax.axis_index("section")
    me = d * n_sec + sec

    w_copies = [
        pltpu.make_async_copy(
            w_ref.at[:, pl.ds(h * half, half)], w_vmem.at[:, pl.ds(h * half, half)], w_sem.at[h]
        )
        for h in range(halves)
    ]
    locals_ = [
        pltpu.make_async_copy(att_ref.at[s], held.at[s, t], local_sem.at[s]) for s in range(steps)
    ]

    def other(k):
        return lax.rem(t + k, n_t)

    def peer(k):
        b = lax.rem(me + k, blocks)
        return b, {"dp": b // n_sec, "section": lax.rem(b, n_sec)}

    barrier = pltpu.get_barrier_semaphore()
    for k in range(1, n_t):
        pl.semaphore_signal(
            barrier, inc=1, device_id={"tensor": other(k)}, device_id_type=MESH
        )
    for k in range(1, blocks):
        pl.semaphore_signal(barrier, inc=1, device_id=peer(k)[1], device_id_type=MESH)
    pl.semaphore_wait(barrier, n_t - 1 + blocks - 1)

    def sends(way, j):
        return (t >= j) & (t < n_t - 1) if way == 0 else (t + j < n_t) & (t > 0)

    def receives(way, j):
        return t - 1 - j >= 0 if way == 0 else t + 1 + j < n_t

    def gather(s, way, j, p):
        at = pl.ds(p * (rows // pieces), rows // pieces)
        block = lax.rem(t - j + n_t, n_t) if way == 0 else lax.rem(t + j, n_t)
        to = lax.rem(t + 1, n_t) if way == 0 else lax.rem(t + n_t - 1, n_t)
        return pltpu.make_async_remote_copy(
            src_ref=att_ref.at[s, at] if j == 0 else held.at[s, block, at],
            dst_ref=held.at[s, block, at],
            send_sem=gs_sem.at[s, way, j, p],
            recv_sem=gr_sem.at[s, way, j, p],
            device_id={"tensor": to},
            device_id_type=MESH,
        )

    def pass_on(s, hops):
        for j in hops:
            for p in range(pieces):
                for way in range(2):

                    @pl.when(receives(way, j))
                    def _(s=s, way=way, j=j, p=p):
                        gather(s, way, j, p).wait_recv()

                    if j + 1 < n_t - 1:

                        @pl.when(sends(way, j + 1))
                        def _(s=s, way=way, j=j, p=p):
                            gather(s, way, j + 1, p).start()

    width = lm_all.shape[-1]
    chosen = choose_ref.shape[1]

    def columns(b):
        return pl.ds(pl.multiple_of(lax.rem(b, n_sec) * width, width), width)

    def send_lm(k):
        b, to = peer(k)
        return pltpu.make_async_remote_copy(
            src_ref=lm_ref.at[:, :, columns(b)], dst_ref=lm_all.at[me],
            send_sem=lms_sem.at[k - 1], recv_sem=lmr_sem.at[k - 1],
            device_id=to, device_id_type=MESH,
        )

    def send_pair(a, s, k):
        b, to = peer(k)
        at = pl.ds(s * chosen, chosen)
        return pltpu.make_async_remote_copy(
            src_ref=pair_ref.at[a, at, columns(b)], dst_ref=pair_all.at[me, a, at],
            send_sem=ps_sem.at[a, s, k - 1], recv_sem=pr_sem.at[a, s, k - 1],
            device_id=to, device_id_type=MESH,
        )

    def rows_of(i, q):
        b = lax.rem(d + i, n_dp) * n_sec + lax.rem(sec + q, n_sec)
        return pl.ds(pl.multiple_of(b * owned, owned), owned)

    def to_section(s, h, q):
        return pltpu.make_async_remote_copy(
            src_ref=part.at[s % 2, h, q - 1],
            dst_ref=got.at[s, h, q - 1],
            send_sem=rs_sem.at[s, h, q - 1],
            recv_sem=rr_sem.at[s, h, q - 1],
            device_id={"section": lax.rem(sec + q, n_sec)},
            device_id_type=MESH,
        )

    def to_dp(s, h, i):
        return pltpu.make_async_remote_copy(
            src_ref=part_dp.at[s % 2, h, i - 1],
            dst_ref=got_dp.at[s, h, i - 1],
            send_sem=ds_sem.at[s, h, i - 1],
            recv_sem=dr_sem.at[s, h, i - 1],
            device_id={"dp": lax.rem(d + i, n_dp)},
            device_id_type=MESH,
        )

    def add_sections(s, h):
        for q in range(1, n_sec):
            to_section(s, h, q).wait_recv()
        for c in range(0, half, tile):
            at, wide = pl.ds(c, tile), pl.ds(h * half + c, tile)
            for i in range(n_dp):
                total = own[s % 2, i, :, wide]
                for q in range(1, n_sec):
                    total += got[s, h, q - 1, i, :, at].astype(F32)
                if i == 0:
                    own[s % 2, 0, :, wide] = total
                else:
                    part_dp[s % 2, h, i - 1, :, at] = total.astype(BF16)
        for i in range(1, n_dp):
            to_dp(s, h, i).start()

    def wait_sent(s):
        for h in range(halves):
            for q in range(1, n_sec):
                to_section(s, h, q).wait_send()
            for i in range(1, n_dp):
                to_dp(s, h, i).wait_send()

    def start_gather(s):
        for way in range(2):

            @pl.when(sends(way, 0))
            def _(s=s, way=way):
                for p in range(pieces):
                    gather(s, way, 0, p).start()

    def finish(s):
        for h in range(halves):
            for i in range(1, n_dp):
                to_dp(s, h, i).wait_recv()
            for c in range(0, half, tile):
                at = pl.ds(h * half + c, tile)
                total = own[s % 2, 0, :, at] + res_ref[s, :, at].astype(F32)
                for i in range(1, n_dp):
                    total += got_dp[s, h, i - 1, :, pl.ds(c, tile)].astype(F32)
                total = total.astype(BF16)
                top_ref[s, :, at] = total
                for a, at_step in ((0, s), (1, s - 1)):
                    if 0 <= at_step < steps - 1:
                        picked = jnp.dot(choose_ref[at_step], total, preferred_element_type=F32)
                        pair_ref[a, pl.ds(at_step * chosen, chosen), at] = picked.astype(BF16)
        for a, at_step in ((0, s), (1, s - 1)):
            if 0 <= at_step < steps - 1:
                for k in range(1, blocks):
                    send_pair(a, at_step, k).start()

    start_gather(0)
    for c in locals_:
        c.start()
    for c in w_copies:
        c.start()
    for s in range(1, min(ahead, steps)):
        start_gather(s)
    for k in range(1, blocks):
        send_lm(k).start()
    keeps = [pltpu.make_async_copy(lm_ref.at[:, :, columns(me)], lm_all.at[me], keep_sem.at[0])]
    for c in keeps:
        c.start()
    for c in locals_:
        c.wait()
    for s in range(steps):
        pass_on(s, range(0 if s == 0 else 1, n_t - 1))
        if s + ahead < steps:
            start_gather(s + ahead)
        if s == 0:
            for c in w_copies:
                c.wait()
        if s >= 2:
            wait_sent(s - 2)
        for h in range(halves):

            def body(i, _, s=s, h=h):
                at = pl.ds(pl.multiple_of(i * tile, tile), tile)
                wide = pl.ds(pl.multiple_of(h * half + i * tile, tile), tile)
                lhs = held[s].reshape(n_t * rows, depth)
                prod = jnp.dot(lhs, w_vmem[:, wide], preferred_element_type=F32)
                acc[...] = prod
                for i in range(n_dp):
                    own[s % 2, i, :, wide] = acc[rows_of(i, 0), :]
                    for q in range(1, n_sec):
                        part[s % 2, h, q - 1, i, :, at] = acc[rows_of(i, q), :].astype(BF16)
                return 0

            lax.fori_loop(0, half // tile, body, 0)
            for q in range(1, n_sec):
                to_section(s, h, q).start()
            if h > 0:
                add_sections(s, h - 1)
            if h == 0 and s + 1 < steps:
                pass_on(s + 1, range(1))
        add_sections(s, halves - 1)
        if s >= 1:
            finish(s - 1)
    finish(steps - 1)
    for s in range(max(0, steps - 2), steps):
        wait_sent(s)
    last = pltpu.make_async_copy(pair_ref.at[:, :, columns(me)], pair_all.at[me], keep_sem.at[1])
    last.start()
    for s in range(steps):
        for way in range(2):
            for j in range(n_t - 1):

                @pl.when(sends(way, j))
                def _(s=s, way=way, j=j):
                    for p in range(pieces):
                        gather(s, way, j, p).wait_send()

    for k in range(1, blocks):
        send_lm(k).wait()
    for s in range(steps - 1):
        for a in range(2):
            for k in range(1, blocks):
                send_pair(a, s, k).wait()
    for c in keeps + [last]:
        c.wait()


def train_kernel(
    n_t, n_dp, n_sec, scale, pair_ref, lm_ref, down_ref, up_all, up_ref, lm_all, pair_all,
    grad_down_ref, grad_up_ref,
    down, ups, both, both_all, inner, inner_all, lms, pairs,
    in_sem, bs_sem, br_sem, is_sem, ir_sem,
):
    blocks = n_dp * n_sec
    count = pair_ref.shape[1]
    rank_width = up_ref.shape[0]
    width = up_ref.shape[1]
    t = lax.axis_index("tensor")
    section = lax.axis_index("section")
    me = lax.axis_index("dp") * n_sec + section

    loads = [
        pltpu.make_async_copy(up_all, ups, in_sem.at[0]),
        pltpu.make_async_copy(down_ref, down, in_sem.at[1]),
        pltpu.make_async_copy(lm_all, lms, in_sem.at[2]),
        pltpu.make_async_copy(pair_all, pairs, in_sem.at[3]),
    ]
    for c in loads:
        c.start()

    def peer(k):
        b = lax.rem(me + k, blocks)
        return {"dp": b // n_sec, "section": lax.rem(b, n_sec)}

    barrier = pltpu.get_barrier_semaphore()
    for k in range(1, n_t):
        pl.semaphore_signal(
            barrier, inc=1, device_id={"tensor": lax.rem(t + k, n_t)}, device_id_type=MESH
        )
    for k in range(1, blocks):
        pl.semaphore_signal(barrier, inc=1, device_id=peer(k), device_id_type=MESH)
    pl.semaphore_wait(barrier, n_t - 1 + blocks - 1)

    def send_both(r, k):
        return pltpu.make_async_remote_copy(
            src_ref=both.at[r], dst_ref=both_all.at[r, t],
            send_sem=bs_sem.at[r, k - 1], recv_sem=br_sem.at[r, k - 1],
            device_id={"tensor": lax.rem(t + k, n_t)}, device_id_type=MESH,
        )

    def summed(r, value):
        both[r] = value
        both_all[r, t] = value
        for k in range(1, n_t):
            send_both(r, k).start()
        for k in range(1, n_t):
            send_both(r, k).wait()
        total = both_all[r, 0]
        for i in range(1, n_t):
            total += both_all[r, i]
        return total

    def send_inner(r, k):
        return pltpu.make_async_remote_copy(
            src_ref=inner.at[r], dst_ref=inner_all.at[r, me],
            send_sem=is_sem.at[r, k - 1], recv_sem=ir_sem.at[r, k - 1],
            device_id=peer(k), device_id_type=MESH,
        )

    loads[1].wait()
    pre = jnp.dot(pair_ref[0], down[2], preferred_element_type=F32)
    for c in range(2):
        pre += jnp.dot(lm_ref[c], down[c], preferred_element_type=F32)
    pre = summed(0, pre)
    sigma = jax.nn.sigmoid(pre)
    gated = (pre * sigma).astype(BF16)
    inner[0] = gated
    inner_all[0, me] = gated
    for k in range(1, blocks):
        send_inner(0, k).start()
    loads[0].wait()
    back = jnp.zeros((count, rank_width), F32)
    cut = min(1024, width)
    for c in range(0, ups.shape[1], cut):
        part = ups[:, pl.ds(c, cut)]
        pred = jnp.dot(gated, part, preferred_element_type=F32)
        away = ((pred - pair_ref[1, :, pl.ds(c, cut)].astype(F32)) / scale).astype(BF16)
        back += lax.dot_general(
            away, part, (((1,), (1,)), ((), ())), preferred_element_type=F32
        )
    back = summed(1, back)
    dpre = (back * sigma * (1.0 + pre * (1.0 - sigma))).astype(BF16)
    inner[1] = dpre
    inner_all[1, me] = dpre
    for k in range(1, blocks):
        send_inner(1, k).start()
    loads[2].wait()
    loads[3].wait()
    for k in range(1, blocks):
        send_inner(0, k).wait()
        send_inner(1, k).wait()
    rows = blocks * count
    gated = inner_all[0].reshape(rows, rank_width)
    dpre = inner_all[1].reshape(rows, rank_width)
    tile = min(512, width)

    def body(i, _):
        at = pl.ds(pl.multiple_of(i * tile, tile), tile)
        over = (((0,), (0,)), ((), ()))
        pred = jnp.dot(gated, up_ref[:, at], preferred_element_type=F32)
        target = pairs[:, 1, :, at].reshape(rows, tile).astype(F32)
        cotangent = ((pred - target) / scale).astype(BF16)
        grad_up_ref[:, at] = lax.dot_general(
            gated, cotangent, over, preferred_element_type=F32
        ).astype(BF16)
        for c in range(3):
            x = lms[:, c, :, at] if c < 2 else pairs[:, 0, :, at]
            grad_down_ref[c, at, :] = lax.dot_general(
                x.reshape(rows, tile), dpre, over, preferred_element_type=F32
            ).astype(BF16)
        return 0

    lax.fori_loop(0, width // tile, body, 0)


def fits(mesh_shape, attended, w_out, residual):
    whole = attended.shape[1] % 16 == 0 and residual.shape[1] % 32 == 0
    return whole and w_out.shape[1] % 1024 == 0 and min(mesh_shape.values()) > 1


def project_plain(attended, w_out, residual):
    whole = lax.all_gather(attended, "tensor", axis=1, tiled=True)
    partial_rows = jnp.einsum("srj,jk->srk", whole, w_out, preferred_element_type=F32)
    summed = lax.psum_scatter(partial_rows, ("dp", "section"), scatter_dimension=1, tiled=True)
    return (residual.astype(F32) + summed).astype(BF16)


def project(mesh_shape, attended, w_out, residual, choose, low_mid):
    steps, rows, depth = attended.shape
    cols = w_out.shape[1]
    n_t, n_dp, n_sec = mesh_shape["tensor"], mesh_shape["dp"], mesh_shape["section"]
    blocks = n_dp * n_sec
    owned = residual.shape[1]
    count = low_mid.shape[1]
    halves = 2
    half = cols // halves
    dma = pltpu.SemaphoreType.DMA
    hbm, vmem = pl.BlockSpec(memory_space=pl.ANY), pl.BlockSpec(memory_space=pltpu.VMEM)
    spread = jax.ShapeDtypeStruct((blocks, 2, count, cols // n_sec), BF16)
    return pl.pallas_call(
        functools.partial(project_kernel, n_t, n_dp, n_sec),
        out_shape=(
            jax.ShapeDtypeStruct(residual.shape, BF16),
            jax.ShapeDtypeStruct((2, count, cols), BF16),
            spread,
            spread,
        ),
        in_specs=[hbm, hbm, vmem, vmem, hbm],
        out_specs=(vmem, vmem, hbm, hbm),
        scratch_shapes=[
            pltpu.VMEM((steps, n_t, rows, depth), BF16),
            pltpu.VMEM((depth, cols), BF16),
            pltpu.VMEM((n_t * rows, 512), F32),
            pltpu.VMEM((2, halves, n_sec - 1, n_dp, owned, half), BF16),
            pltpu.VMEM((2, n_dp, owned, cols), F32),
            pltpu.VMEM((steps, halves, n_sec - 1, n_dp, owned, half), BF16),
            pltpu.VMEM((2, halves, n_dp - 1, owned, half), BF16),
            pltpu.VMEM((steps, halves, n_dp - 1, owned, half), BF16),
            dma((halves,)),
            dma((steps,)),
            dma((steps, 2, n_t - 1, 2)),
            dma((steps, 2, n_t - 1, 2)),
            dma((steps, halves, n_sec - 1)),
            dma((steps, halves, n_sec - 1)),
            dma((steps, halves, n_dp - 1)),
            dma((steps, halves, n_dp - 1)),
            dma((blocks - 1,)),
            dma((blocks - 1,)),
            dma((2, steps - 1, blocks - 1)),
            dma((2, steps - 1, blocks - 1)),
            dma((2,)),
        ],
        compiler_params=pltpu.CompilerParams(
            collective_id=0, has_side_effects=True, vmem_limit_bytes=62 * 2**20
        ),
        cost_estimate=pl.CostEstimate(
            flops=2 * steps * rows * n_t * depth * cols,
            bytes_accessed=2 * w_out.size,
            transcendentals=0,
        ),
    )(attended, w_out, residual, choose, low_mid)


def train(mesh_shape, scale, pair, low_mid, down_full, up_full, up_map, lm_all, pair_all):
    n_t, n_dp, n_sec = mesh_shape["tensor"], mesh_shape["dp"], mesh_shape["section"]
    blocks = n_dp * n_sec
    count = pair.shape[1]
    rank_width, width = up_map.shape
    dma = pltpu.SemaphoreType.DMA
    hbm, vmem = pl.BlockSpec(memory_space=pl.ANY), pl.BlockSpec(memory_space=pltpu.VMEM)
    return pl.pallas_call(
        functools.partial(train_kernel, n_t, n_dp, n_sec, scale),
        out_shape=(
            jax.ShapeDtypeStruct((3, width, rank_width), BF16),
            jax.ShapeDtypeStruct((rank_width, width), BF16),
        ),
        in_specs=[vmem, vmem, hbm, hbm, vmem, hbm, hbm],
        out_specs=(vmem, vmem),
        scratch_shapes=[
            pltpu.VMEM(down_full.shape, BF16),
            pltpu.VMEM(up_full.shape, BF16),
            pltpu.VMEM((2, count, rank_width), F32),
            pltpu.VMEM((2, n_t, count, rank_width), F32),
            pltpu.VMEM((2, count, rank_width), BF16),
            pltpu.VMEM((2, blocks, count, rank_width), BF16),
            pltpu.VMEM(lm_all.shape, BF16),
            pltpu.VMEM(pair_all.shape, BF16),
            dma((4,)),
            dma((2, n_t - 1)),
            dma((2, n_t - 1)),
            dma((2, blocks - 1)),
            dma((2, blocks - 1)),
        ],
        compiler_params=pltpu.CompilerParams(
            collective_id=1, has_side_effects=True, vmem_limit_bytes=48 * 2**20
        ),
    )(pair, low_mid, down_full, up_full, up_map, lm_all, pair_all)


def on_device(
    mesh_shape, queries, cache, fresh_kv, lengths, w_out, residual, layers, accepted, down_map, up_map
):
    steps = queries.shape[0]
    n_t, n_dp, n_sec = mesh_shape["tensor"], mesh_shape["dp"], mesh_shape["section"]
    blocks = n_dp * n_sec
    owned = residual.shape[1]
    section = lax.axis_index("section")
    rank_width = up_map.shape[0]
    col_width = up_map.shape[1]

    kernels = fits(mesh_shape, queries, w_out, residual)
    most = 32 if kernels else min(MOST, owned)
    mine = lax.dynamic_slice_in_dim(accepted, section * owned, owned, axis=1)[: steps - 1]
    place = jnp.cumsum(mine, axis=1) - 1
    choose = (place[:, None, :] == jnp.arange(most)[None, :, None]) & (mine[:, None, :] > 0)
    choose = choose.astype(BF16)
    count = (steps - 1) * most

    def compact(x):
        picked = jnp.einsum("smr,srj->smj", choose, x, preferred_element_type=F32)
        return picked.astype(BF16).reshape(count, x.shape[-1])

    def swap(x, k):
        pairs = [(b, (b + k) % blocks) for b in range(blocks)]
        return lax.ppermute(x, ("dp", "section"), pairs)

    def half_for(x, k):
        b = (me + k) % blocks
        return lax.dynamic_slice_in_dim(x, (b % n_sec) * col_width, col_width, axis=x.ndim - 1)

    low_mid = jnp.stack([compact(layers[c, : steps - 1]) for c in range(2)])
    me = lax.axis_index("dp") * n_sec + section

    def in_order(pieces):
        axis = pieces[0].ndim - 2
        size = pieces[0].shape[axis]
        shape = list(pieces[0].shape)
        shape[axis] = blocks * size
        laid = jnp.zeros(shape, pieces[0].dtype)
        for k, piece in enumerate(pieces):
            b = (me + blocks - k) % blocks
            laid = lax.dynamic_update_slice_in_dim(laid, piece, b * size, axis=axis)
        return laid

    down_full = lax.all_gather(down_map, "section", axis=1, tiled=True)
    up_full = lax.all_gather(up_map, "section", axis=1, tiled=True)
    gram = jnp.einsum("kj,lj->kl", up_map, up_map, preferred_element_type=F32)
    queries, low_mid = lax.optimization_barrier((queries, low_mid))
    attended = attend(queries, cache, fresh_kv, lengths)
    if kernels:
        top_hidden, pair, lm_all, pair_all = project(
            mesh_shape, attended, w_out, residual, choose, low_mid
        )
        grad_down, grad_up = train(
            mesh_shape, steps - 1, pair, low_mid, down_full, up_full, up_map, lm_all, pair_all
        )
        return top_hidden, grad_down, grad_up

    low_mid_all = in_order(
        [half_for(low_mid, 0)] + [swap(half_for(low_mid, k), k) for k in range(1, blocks)]
    )
    gram = lax.psum(gram, ("tensor", "section"))
    pre_early = jnp.einsum("cnj,cjk->nk", low_mid, down_full[:2], preferred_element_type=F32)

    top_hidden = project_plain(attended, w_out, residual)

    top = compact(top_hidden[: steps - 1])
    target = compact(top_hidden[1:])
    pair = jnp.stack([top, target])
    pair_all = in_order([half_for(pair, 0)] + [swap(half_for(pair, k), k) for k in range(1, blocks)])

    pre_part = pre_early + jnp.dot(top, down_full[2], preferred_element_type=F32)
    goal_part = jnp.einsum("nj,kj->nk", target, up_full, preferred_element_type=F32)
    both = jnp.concatenate([pre_part, goal_part], axis=1)
    if n_t <= 4:
        total = both
        for k in range(1, n_t):
            pairs = [(a, (a + k) % n_t) for a in range(n_t)]
            total = total + lax.ppermute(both, "tensor", pairs)
        both = total
    else:
        both = lax.psum(both, "tensor")
    pre, goal = both[:, :rank_width], both[:, rank_width:]
    sigma = jax.nn.sigmoid(pre)
    gated = (pre * sigma).astype(BF16)
    back = jnp.dot(gated.astype(F32), gram, precision=lax.Precision.HIGHEST) - goal
    back = back / (steps - 1)
    dpre = (back * sigma * (1.0 + pre * (1.0 - sigma))).astype(BF16)
    inner = jnp.concatenate([gated, dpre], axis=1)
    inner_all = in_order([inner] + [swap(inner, k) for k in range(1, blocks)])
    gated, dpre = inner_all[:, :rank_width], inner_all[:, rank_width:]

    pred = jnp.dot(gated, up_map, preferred_element_type=F32)
    cotangent = ((pred - pair_all[1].astype(F32)) / (steps - 1)).astype(BF16)
    grad_up = jnp.einsum("nk,nj->kj", gated, cotangent, preferred_element_type=F32).astype(BF16)
    grad_down = jnp.stack(
        [
            jnp.einsum("nj,nk->jk", x, dpre, preferred_element_type=F32).astype(BF16)
            for x in (low_mid_all[0], low_mid_all[1], pair_all[0])
        ]
    )
    return top_hidden, grad_down, grad_up


def solution(mesh):
    placed = (
        P("groups", "tensor", ("dp", "section")),
        P("groups", ("dp", "section"), "tensor", None, None),
        P("groups", None, ("dp", "section"), "tensor", None),
        P(("groups", "tensor")),
        P(("dp", "section"), "tensor"),
        P("groups", ("dp", "section"), "tensor"),
        P("groups", None, ("dp", "section"), "tensor"),
        P("groups", "dp"),
        P(None, ("tensor", "section"), None),
        P(None, ("tensor", "section")),
    )
    return jax.shard_map(
        functools.partial(on_device, dict(mesh.shape)),
        mesh=mesh,
        in_specs=placed,
        out_specs=(
            P("groups", ("dp", "section"), "tensor"),
            P("groups", ("tensor", "section"), None),
            P("groups", ("tensor", "section")),
        ),
        check_vma=False,
    )
```
